512 devices in a mesh: serve: 64 (over y, z), head: 8 (over x, core).
Axes of the slice: x: 4, y: 4, z: 16, core: 2. Of those that a mesh axis runs over, the one named last changes fastest.
Arguments:
- queries: bfloat16 [2, 2048, 8192], P(None, ('serve', 'head')), may hold values from -5 to 5
- new_kv: bfloat16 [2, 2048, 2048], P(None, ('serve', 'head')), may hold values from -5 to 5
- suffix_kv: bfloat16 [2048, 8, 2, 128, 128], P('serve', 'head'), may hold values from -5 to 5
- prefix_kv: bfloat16 [128, 8, 2, 2048, 128], P('serve', 'head'), may hold values from -5 to 5
- owner_map: int32 [32, 2], replicated, may hold values from 0 to 127, as said below
- host_slot: int32 [2048], replicated, may hold values from 0 to 2047, as said below
- suffix_len: int32 [2048], replicated, may hold values from 1 to 128, 131072 in all
Outputs:
- attended: bfloat16 [2, 2048, 8192], P(None, ('serve', 'head'))
The draws below stay inside these ranges and needn't reach their ends.
Inputs may be any that keep to these rules, and one draw needn't show every extreme that they name: `owner_map`: an entry is device * 2 + slot on the serve axis; no slot is named twice; the two halves of a prompt lie on different devices; 16 devices hold two slabs, 32 hold one and the rest none. `host_slot`: every slot holds one sample; the samples of every prompt are spread evenly, 1 to each serve device; slot g lies on serve device g // 32.
All inputs are finite; a program needn't handle non-finite values.
Results may differ from the reference program's by a relative error of at most 0.0047.
Values may be sent and summed in bfloat16 or wider, within the bound.
A program may use at most 64 MiB of HBM per device.

```python
import math
import jax
import jax.numpy as jnp
import numpy as np
from jax import lax

HD = 128
QH = 64
KVH = 8
SPP = 64
SUF = 128
STEPS = 2
SLOTS = 2
SLAB = 2048
PROMPTS = 32
SAMPLES = 2048
HOST = 32
N_SERVE = 64


def owner_slabs(key):
    key = jax.random.fold_in(key, 7)
    first_key, second_key, third_key, fourth_key = jax.random.split(key, 4)
    quarter = PROMPTS // 2
    device_order = jax.random.permutation(first_key, 2 * PROMPTS).astype(jnp.int32)
    rank_values = jnp.arange(PROMPTS, dtype=jnp.int32)
    heavy_slab = device_order[rank_values // 2] * SLOTS + rank_values % 2
    light_choice = jax.random.randint(third_key, (PROMPTS,), 0, SLOTS)
    light_slab = device_order[quarter + rank_values] * SLOTS + light_choice
    flipped = jax.random.randint(fourth_key, (PROMPTS,), 0, 2) == 1
    first_half = jnp.where(flipped, light_slab, heavy_slab)
    second_half = jnp.where(flipped, heavy_slab, light_slab)
    paired = jnp.stack([first_half, second_half], axis=1).astype(jnp.int32)
    shuffled = jax.random.permutation(second_key, PROMPTS)
    return jnp.zeros((PROMPTS, 2), jnp.int32).at[shuffled].set(paired)


def host_slots(key):
    key = jax.random.fold_in(key, 9)
    first_key, second_key = jax.random.split(key)
    repeats = SPP // (2 * PROMPTS)
    orders = jax.vmap(lambda subkey: jax.random.permutation(subkey, SPP))(jax.random.split(first_key, PROMPTS)).astype(jnp.int32)
    device_of = orders // repeats
    pre_slot = jnp.arange(PROMPTS, dtype=jnp.int32)[:, None] * repeats + orders % repeats
    shuffles = jax.vmap(lambda subkey: jax.random.permutation(subkey, HOST))(jax.random.split(second_key, 2 * PROMPTS)).astype(jnp.int32)
    local_slot = shuffles[device_of, pre_slot]
    return (device_of * HOST + local_slot).reshape(-1).astype(jnp.int32)


def draw_queries(key, part):
    key = jax.random.fold_in(key, 1)
    shape_full = (STEPS, SAMPLES, KVH, QH // KVH, HD)
    values_drawn = jnp.clip(jax.random.normal(key, shape_full, jnp.float32), -5.0, 5.0)
    return values_drawn.reshape(STEPS, SAMPLES, QH * HD).astype(jnp.bfloat16)


def draw_new_kv(key, part):
    key = jax.random.fold_in(key, 2)
    shape_full = (STEPS, SAMPLES, KVH, 2, HD)
    values_drawn = jnp.clip(jax.random.normal(key, shape_full, jnp.float32), -5.0, 5.0)
    return values_drawn.reshape(STEPS, SAMPLES, KVH * 2 * HD).astype(jnp.bfloat16)


def draw_suffix_kv(key, part):
    key = jax.random.fold_in(key, 3)
    shape_full = (SAMPLES, KVH, 2, SUF, HD)
    values_drawn = jnp.clip(jax.random.normal(key, shape_full, jnp.float32), -5.0, 5.0)
    return values_drawn.astype(jnp.bfloat16)


def draw_prefix_kv(key, part):
    key = jax.random.fold_in(key, 4)
    slab_total = N_SERVE * SLOTS

    def one_slab(slab):
        slab_key = jax.random.fold_in(key, slab)
        draw_key = jax.random.fold_in(slab_key, 0)
        values_drawn = jnp.clip(jax.random.normal(draw_key, (KVH, 2, SLAB, HD), jnp.float32), -5.0, 5.0)
        return values_drawn.astype(jnp.bfloat16)
    return lax.map(one_slab, jnp.arange(slab_total, dtype=jnp.int32))


def draw_owner_map(key, part):
    return owner_slabs(key)


def draw_host_slot(key, part):
    return host_slots(key)


def split_up(amount, total, bound, lean):
    weights = [(1 << 20) // math.isqrt(rank ** lean) + 1 for rank in range(2, amount + 1)]
    rest, given = total - bound - (amount - 1), [1] * (amount - 1)
    while rest > 0:
        movable = [i for i in range(amount - 1) if given[i] < bound]
        mass, left = sum([weights[i] for i in movable]), rest
        for i in movable:
            addition = min(bound - given[i], max(1, left * weights[i] // mass), rest)
            given[i] = given[i] + addition
            rest = rest - addition
    return np.array([bound] + given)


def ragged_sizes(rng, amount, total, limit, skew):
    if amount == 2:
        one = jax.random.randint(rng, (), max(1, total - limit), min(limit, total - 1) + 1)
        return jnp.stack([one, total - one])
    tallies = jnp.asarray(split_up(amount, total, limit, skew), jnp.int32)
    couples = (amount - 1) // 2
    donor, taker = tallies[1:1 + 2 * couples:2], tallies[2:2 + 2 * couples:2]
    slack = jnp.minimum(donor - 1, limit - taker)
    passed = jax.random.randint(jax.random.fold_in(rng, 1), (couples,), 0, 1 << 20) % (slack + 1)
    tallies = tallies.at[1:1 + 2 * couples:2].set(donor - passed).at[2:2 + 2 * couples:2].set(taker + passed)
    return tallies[jax.random.permutation(jax.random.fold_in(rng, 2), amount)]


def setup_inputs(seed: int = 0) -> dict:
    seeds = jax.random.split(jax.random.key(seed), 8)
    queries = draw_queries(jax.random.fold_in(seeds[7], 71), 0)
    new_kv = draw_new_kv(jax.random.fold_in(seeds[7], 71), 0)
    suffix_kv = draw_suffix_kv(jax.random.fold_in(seeds[7], 71), 0)
    prefix_kv = draw_prefix_kv(jax.random.fold_in(seeds[7], 71), 0)
    owner_map = draw_owner_map(jax.random.fold_in(seeds[7], 71), 0)
    host_slot = draw_host_slot(jax.random.fold_in(seeds[7], 71), 0)
    suffix_len = ragged_sizes(seeds[6], SAMPLES, SAMPLES * SUF // 2, SUF, 2).astype(jnp.int32)
    return {"queries": queries, "new_kv": new_kv, "suffix_kv": suffix_kv, "prefix_kv": prefix_kv, "owner_map": owner_map, "host_slot": host_slot, "suffix_len": suffix_len}


def settle(scores):
    maximum = jnp.max(scores, axis=-1, keepdims=True)
    exponent = jnp.exp(scores - maximum)
    totals = jnp.sum(exponent, axis=-1)
    weights = lax.optimization_barrier(exponent.astype(jnp.bfloat16)).astype(jnp.float32)
    return maximum[..., 0], totals, weights


def reference(queries, new_kv, suffix_kv, prefix_kv, owner_map, host_slot, suffix_len):
    per_group = QH // KVH
    score_scale = HD ** -0.5

    def one_prompt(prompt):
        slots = lax.dynamic_slice_in_dim(host_slot, prompt * SPP, SPP)
        lengths = lax.dynamic_slice_in_dim(suffix_len, prompt * SPP, SPP)
        query = jnp.take(queries, slots, axis=1).astype(jnp.float32).reshape(STEPS, SPP, KVH, per_group, HD)
        part_outs = []
        part_logs = []
        for half_index in range(2):
            slab_kv = jnp.take(prefix_kv, owner_map[prompt, half_index], axis=0).astype(jnp.float32)
            scores = jnp.einsum("tscgd,ckd->tscgk", query, slab_kv[:, 0]) * score_scale
            maximum, totals, weights = settle(scores)
            blended = jnp.einsum("tscgk,ckd->tscgd", weights, slab_kv[:, 1]) / totals[..., None]
            part_outs.append(blended)
            part_logs.append(maximum + jnp.log(totals))
        cache = jnp.take(suffix_kv, slots, axis=0).astype(jnp.float32)
        fresh = jnp.take(new_kv, slots, axis=1).astype(jnp.float32).reshape(STEPS, SPP, KVH, 2, HD)
        fresh_keys = jnp.transpose(fresh[:, :, :, 0], (1, 2, 0, 3))
        fresh_values = jnp.transpose(fresh[:, :, :, 1], (1, 2, 0, 3))
        all_keys = jnp.concatenate([cache[:, :, 0], fresh_keys], axis=2)
        all_values = jnp.concatenate([cache[:, :, 1], fresh_values], axis=2)
        scores = jnp.einsum("tscgd,sckd->tscgk", query, all_keys) * score_scale
        cache_live = jnp.arange(SUF, dtype=jnp.int32)[None, :] < lengths[:, None]
        cache_live = jnp.broadcast_to(cache_live[None], (STEPS, SPP, SUF))
        fresh_live = jnp.arange(STEPS, dtype=jnp.int32)[None, :] <= jnp.arange(STEPS, dtype=jnp.int32)[:, None]
        fresh_live = jnp.broadcast_to(fresh_live[:, None, :], (STEPS, SPP, STEPS))
        live_keys = jnp.concatenate([cache_live, fresh_live], axis=2)
        scores = jnp.where(live_keys[:, :, None, None, :], scores, -jnp.inf)
        maximum, totals, weights = settle(scores)
        own_out = jnp.einsum("tscgk,sckd->tscgd", weights, all_values) / totals[..., None]
        own_log = maximum + jnp.log(totals)
        highest = jnp.maximum(jnp.maximum(part_logs[0], part_logs[1]), own_log)
        factors = [jnp.exp(part_logs[0] - highest), jnp.exp(part_logs[1] - highest), jnp.exp(own_log - highest)]
        numerator = factors[0][..., None] * part_outs[0] + factors[1][..., None] * part_outs[1] + factors[2][..., None] * own_out
        denominator = factors[0] + factors[1] + factors[2]
        return (numerator / denominator[..., None]).astype(jnp.bfloat16).reshape(STEPS, SPP, QH * HD)

    results = lax.map(one_prompt, jnp.arange(PROMPTS, dtype=jnp.int32))
    flat = jnp.swapaxes(results, 0, 1).reshape(STEPS, SAMPLES, QH * HD)
    return jnp.zeros((STEPS, SAMPLES, QH * HD), jnp.bfloat16).at[:, host_slot].set(flat)
```

```python
import functools

import jax
import jax.numpy as jnp
from jax import lax
from jax.experimental import pallas as pl
from jax.experimental.pallas import tpu as pltpu
from jax.sharding import PartitionSpec as P

NZ = 16
G = 8
MESH = pl.DeviceIdType.MESH
F32 = jnp.float32
BF16 = jnp.bfloat16
LOG2E = 1.4426950408889634


def dot(a, b, dims):
    return lax.dot_general(a, b, (dims, ((), ())), preferred_element_type=F32)


def wait_bytes(ref, sem):
    pltpu.make_async_copy(ref, ref, sem).wait()


def kernel(
    cfg,
    q_ref, fresh_ref, slot_ref, len_ref, owner_ref, suffix_ref, prefix_ref,
    out_ref,
    stage, hsend, hin, table_v, table_s, qsend, qin, osend, oin, lsend, lin,
    suffix, prefix, own_out, own_lse, asend, ain, scores,
    prefix_sem, suffix_sem, table_sem, hsend_sem, hrecv_sem, qsend_sem, qrecv_sem,
    osend_sem, orecv_sem, lsend_sem, lrecv_sem, asend_sem, arecv_sem,
):
    steps, per, heads, ny, nz, prompts, slab = cfg
    serve = ny * nz
    host = per * heads
    hd = 128
    rows = steps * G
    me_s = lax.axis_index("serve")
    me_h = lax.axis_index("head")
    my_y, my_z = me_s // nz, me_s % nz
    scale = hd**-0.5

    def ahead(shift):
        y, z = (my_y + shift // nz) % ny, (my_z + shift % nz) % nz
        return y * nz + z

    def behind(shift):
        y, z = (my_y - shift // nz + ny) % ny, (my_z - shift % nz + nz) % nz
        return y * nz + z

    barrier = pltpu.get_barrier_semaphore()

    def greet_serve(i, _):
        pl.semaphore_signal(barrier, inc=1, device_id=(ahead(i), me_h), device_id_type=MESH)
        return 0

    def greet_head(i, _):
        pl.semaphore_signal(
            barrier, inc=1, device_id=(me_s, (me_h + i) % heads), device_id_type=MESH
        )
        return 0

    if heads > 1:
        lax.fori_loop(1, heads, greet_head, 0)
    lax.fori_loop(1, serve, greet_serve, 0)

    prefix_copy = pltpu.make_async_copy(prefix_ref, prefix, prefix_sem)
    suffix_copy = pltpu.make_async_copy(suffix_ref, suffix, suffix_sem)
    prefix_copy.start()
    suffix_copy.start()

    lane = lax.broadcasted_iota(jnp.int32, (host, 128), 1)
    sub = lax.broadcasted_iota(jnp.int32, (host, 128), 0)
    wanted = sub + me_s * host
    found = jnp.zeros((host, 128), jnp.int32)
    for r in range(slot_ref.shape[0]):
        here = jnp.broadcast_to(slot_ref[r : r + 1, :], (host, 128)) == wanted
        held = (r * 128 + lane) // serve * 256 + jnp.broadcast_to(len_ref[r : r + 1, :], (host, 128))
        found = found + jnp.where(here, held, 0)
    found = jnp.broadcast_to(jnp.sum(found, axis=1, keepdims=True), (host, 128))
    prompt_of = found // 256
    length_of = found - prompt_of * 256
    halves = []
    for i in range(2):
        half = jnp.zeros((host, 128), jnp.int32)
        for p in range(prompts):
            half = jnp.where(prompt_of == p, owner_ref[p, i], half)
        halves.append(half)
    sent = jnp.where((halves[0] == lane) | (halves[1] == lane), sub, 0)
    table_v[0:host, :] = jnp.where(
        lane == 0, halves[0], jnp.where(lane == 1, halves[1], length_of)
    )
    table_v[host : host + 8, :] = jnp.broadcast_to(jnp.max(sent, axis=0, keepdims=True), (8, 128))
    table_copy = pltpu.make_async_copy(table_v, table_s, table_sem)
    table_copy.start()

    for t in range(steps):
        wide = q_ref[t].astype(F32)
        for c in range(heads):
            for g in range(G):
                col = (c * G + g) * hd
                stage[c, pl.ds(t * G + g, per, stride=rows), :] = wide[:, col : col + hd]
        wide = fresh_ref[t].astype(F32)
        for c in range(heads):
            for kv in range(2):
                base = per * rows + kv * rows
                col = (2 * c + kv) * hd
                stage[c, pl.ds(base + t, per, stride=steps), :] = wide[:, col : col + hd]
    used = per * steps
    for c in range(heads):
        for kv in range(2):
            base = per * rows + kv * rows
            stage[c, base + used : base + rows, :] = jnp.zeros((rows - used, hd), F32)
        hsend[c] = stage[c].astype(BF16).reshape(per + 2, rows, hd)

    pl.semaphore_wait(barrier, serve - 1 + heads - 1)

    def send_head(i, _):
        c = (me_h + i) % heads
        pltpu.make_async_remote_copy(
            src_ref=hsend.at[c],
            dst_ref=hin.at[me_h],
            send_sem=hsend_sem,
            recv_sem=hrecv_sem,
            device_id=(me_s, c),
            device_id_type=MESH,
        ).start()
        return 0

    if heads > 1:
        lax.fori_loop(1, heads, send_head, 0)
    hin[me_h] = hsend[me_h]
    table_copy.wait()
    if heads > 1:
        wait_bytes(hin.at[pl.ds(0, heads - 1)], hrecv_sem)

    def gather(shift, d):
        for j in range(2):
            k = table_s[host, d * 2 + j]
            qsend[shift, j] = hin[k // per, k % per]

    gather(0, me_s)
    qin[0] = qsend[0]

    def send_queries(shift, _):
        d = ahead(shift)
        gather(shift, d)
        pltpu.make_async_remote_copy(
            src_ref=qsend.at[shift],
            dst_ref=qin.at[shift],
            send_sem=qsend_sem,
            recv_sem=qrecv_sem.at[shift // nz],
            device_id=(d, me_h),
            device_id_type=MESH,
        ).start()
        return 0

    lax.fori_loop(1, serve, send_queries, 0)

    suffix_copy.wait()
    col = lax.broadcasted_iota(jnp.int32, (host * rows, heads * rows), 1)
    row = lax.broadcasted_iota(jnp.int32, (host * rows, heads * rows), 0)
    col_sample = col // rows * per + col % rows // steps
    live = (
        (col_sample == row // rows) & (col % rows < used) & (col % steps <= row % rows // G)
    )
    q_all = hin[:, 0:per].reshape(host * rows, hd)
    fresh_k = hin[:, per].reshape(heads * rows, hd)
    fresh_v = hin[:, per + 1].reshape(heads * rows, hd)
    fresh_scores = jnp.where(live, dot(q_all, fresh_k, ((1,), (1,))), -jnp.inf)
    lanes16 = lax.broadcasted_iota(jnp.int32, (rows, 128), 1)

    def own_scores(k, _):
        s = dot(hin[k // per, k % per], suffix[k, 0], ((1,), (1,)))
        scores[k] = jnp.where(lanes16 < table_s[k, 2], s, -jnp.inf)
        return 0

    lax.fori_loop(0, host, own_scores, 0)
    cache_scores = scores[...].reshape(host * rows, 128)
    top = jnp.maximum(
        jnp.max(cache_scores, axis=1, keepdims=True), jnp.max(fresh_scores, axis=1, keepdims=True)
    )
    cache_exp = jnp.exp((cache_scores - top) * scale)
    fresh_exp = jnp.exp((fresh_scores - top) * scale)
    total = jnp.sum(cache_exp, axis=1, keepdims=True) + jnp.sum(fresh_exp, axis=1, keepdims=True)
    scores[...] = cache_exp.reshape(host, rows, 128)
    own_out[...] = dot(fresh_exp.astype(BF16), fresh_v, ((1,), (0,))).reshape(host, rows, hd)
    own_lse[...] = jnp.broadcast_to(top * scale + jnp.log(total), (host * rows, 128)).reshape(
        host, rows, 128
    )
    inverse = jnp.broadcast_to(1.0 / total, (host * rows, 128)).reshape(host, rows, 128)

    def own_values(k, _):
        own_out[k] = own_out[k] + dot(scores[k].astype(BF16), suffix[k, 1], ((1,), (0,)))
        return 0

    lax.fori_loop(0, host, own_values, 0)
    own_out[...] = own_out[...] * inverse

    prefix_copy.wait()
    tile = nz * rows

    def group(r, _):
        @pl.when(r == 0)
        def _():
            wait_bytes(qin.at[pl.ds(1, nz - 1)], qrecv_sem.at[0])

        @pl.when(r > 0)
        def _():
            wait_bytes(qin.at[pl.ds(0, nz)], qrecv_sem.at[r])

        first = r * nz

        def half(j, _):
            q = qin[pl.ds(first, nz), j].reshape(tile, hd)
            s = dot(q, prefix[j, 0], ((1,), (1,)))
            top = jnp.max(s, axis=1, keepdims=True)
            p = jnp.exp2(s * (scale * LOG2E) - top * (scale * LOG2E))
            total = jnp.sum(p, axis=1, keepdims=True)
            o = dot(p.astype(BF16), prefix[j, 1], ((1,), (0,))) / total
            osend[pl.ds(first, nz), j] = o.astype(BF16).reshape(nz, rows, hd)
            lse = jnp.broadcast_to(top * scale + jnp.log(total), (tile, 128))
            for b in range(tile // 128):
                flat = jnp.transpose(lse[b * 128 : (b + 1) * 128, :])
                lsend[r * (tile // 128) + b, pl.ds(j, 1), :] = flat[0:1, :]
            return 0

        lax.fori_loop(0, 2, half, 0)

        def send_back(shift, _):
            @pl.when(shift > 0)
            def _():
                d = behind(shift)
                pltpu.make_async_remote_copy(
                    src_ref=osend.at[shift],
                    dst_ref=oin.at[shift],
                    send_sem=osend_sem,
                    recv_sem=orecv_sem,
                    device_id=(d, me_h),
                    device_id_type=MESH,
                ).start()
                pltpu.make_async_remote_copy(
                    src_ref=lsend.at[shift // 8],
                    dst_ref=lin.at[shift],
                    send_sem=lsend_sem,
                    recv_sem=lrecv_sem,
                    device_id=(d, me_h),
                    device_id_type=MESH,
                ).start()

            return 0

        lax.fori_loop(first, first + nz, send_back, 0)
        return 0

    lax.fori_loop(0, ny, group, 0)
    oin[0] = osend[0]
    lin[0] = lsend[0]
    wait_bytes(lin.at[pl.ds(1, serve - 1)], lrecv_sem)
    wait_bytes(oin.at[pl.ds(1, serve - 1)], orecv_sem)

    sub16 = lax.broadcasted_iota(jnp.int32, (rows, 128), 0)

    def combine(k, _):
        outs, logs = [], []
        for i in range(2):
            h = table_s[k, i]
            d, j = h // 2, h % 2
            z = (d % nz - my_z + nz) % nz
            shift = (d // nz - my_y + ny) % ny * nz + z
            outs.append(oin[shift, j].astype(F32))
            line = jnp.broadcast_to(lin[shift, pl.ds(j, 1), :], (rows, 128))
            mine = lanes16 == sub16 + z % 8 * rows
            logs.append(jnp.sum(jnp.where(mine, line, 0.0), axis=1, keepdims=True))
        own = own_lse[k]
        top = jnp.maximum(jnp.maximum(logs[0], logs[1]), own)
        a0, a1, a2 = jnp.exp(logs[0] - top), jnp.exp(logs[1] - top), jnp.exp(own - top)
        mixed = (a0 * outs[0] + a1 * outs[1] + a2 * own_out[k]) / (a0 + a1 + a2)
        asend[k // per, k % per] = mixed.astype(BF16)
        return 0

    lax.fori_loop(0, host, combine, 0)

    def send_out(i, _):
        c = (me_h + i) % heads
        pltpu.make_async_remote_copy(
            src_ref=asend.at[c],
            dst_ref=ain.at[me_h],
            send_sem=asend_sem,
            recv_sem=arecv_sem,
            device_id=(me_s, c),
            device_id_type=MESH,
        ).start()
        return 0

    if heads > 1:
        lax.fori_loop(1, heads, send_out, 0)
    ain[me_h] = asend[me_h]
    if heads > 1:
        wait_bytes(ain.at[pl.ds(0, heads - 1)], arecv_sem)
    for c in range(heads):
        stage[c, 0 : per * rows, :] = ain[c].astype(F32).reshape(per * rows, hd)
    for t in range(steps):
        for c in range(heads):
            for g in range(G):
                col = (c * G + g) * hd
                out_ref[t, :, col : col + hd] = stage[
                    c, pl.ds(t * G + g, per, stride=rows), :
                ].astype(BF16)

    wait_bytes(qsend.at[pl.ds(0, serve - 1)], qsend_sem)
    wait_bytes(osend.at[pl.ds(0, serve - 1)], osend_sem)
    wait_bytes(lin.at[pl.ds(0, serve - 1)], lsend_sem)
    if heads > 1:
        wait_bytes(hsend.at[pl.ds(0, heads - 1)], hsend_sem)
        wait_bytes(asend.at[pl.ds(0, heads - 1)], asend_sem)


def local(queries, new_kv, suffix_kv, prefix_kv, owner_map, host_slot, suffix_len):
    serve, heads = lax.axis_size("serve"), lax.axis_size("head")
    steps, per = queries.shape[0], queries.shape[1]
    host, slab = suffix_kv.shape[0], prefix_kv.shape[3]
    nz = NZ
    ny = serve // nz
    rows, hd = steps * G, 128
    cfg = (steps, per, heads, ny, nz, owner_map.shape[0], slab)
    dma = pltpu.SemaphoreType.DMA
    vmem = pl.BlockSpec(memory_space=pltpu.VMEM)
    smem = pl.BlockSpec(memory_space=pltpu.SMEM)
    hbm = pl.BlockSpec(memory_space=pltpu.HBM)
    return pl.pallas_call(
        functools.partial(kernel, cfg),
        out_shape=jax.ShapeDtypeStruct(queries.shape, BF16),
        in_specs=[vmem, vmem, vmem, vmem, smem, hbm, hbm],
        out_specs=vmem,
        scratch_shapes=[
            pltpu.VMEM((heads, (per + 2) * rows, hd), F32),
            pltpu.VMEM((heads, per + 2, rows, hd), BF16),
            pltpu.VMEM((heads, per + 2, rows, hd), BF16),
            pltpu.VMEM((host + 8, 128), jnp.int32),
            pltpu.SMEM((host + 8, 128), jnp.int32),
            pltpu.VMEM((serve, 2, rows, hd), BF16),
            pltpu.VMEM((serve, 2, rows, hd), BF16),
            pltpu.VMEM((serve, 2, rows, hd), BF16),
            pltpu.VMEM((serve, 2, rows, hd), BF16),
            pltpu.VMEM((serve // 8, 2, 128), F32),
            pltpu.VMEM((serve, 2, 128), F32),
            pltpu.VMEM((host, 2, 128, hd), BF16),
            pltpu.VMEM((2, 2, slab, hd), BF16),
            pltpu.VMEM((host, rows, hd), F32),
            pltpu.VMEM((host, rows, 128), F32),
            pltpu.VMEM((heads, per, rows, hd), BF16),
            pltpu.VMEM((heads, per, rows, hd), BF16),
            pltpu.VMEM((host, rows, 128), F32),
            dma, dma, dma, dma, dma, dma, dma((ny,)), dma, dma, dma, dma, dma, dma,
        ],
        compiler_params=pltpu.CompilerParams(
            collective_id=0, has_side_effects=True, vmem_limit_bytes=56 * 1024 * 1024
        ),
    )(
        queries,
        new_kv,
        host_slot.reshape(-1, 128),
        suffix_len.reshape(-1, 128),
        owner_map,
        suffix_kv.reshape(host, 2, 128, hd),
        prefix_kv.reshape(2, 2, slab, hd),
    )


def solution(mesh):
    return jax.shard_map(
        local,
        mesh=mesh,
        in_specs=(
            P(None, ("serve", "head"), None),
            P(None, ("serve", "head"), None),
            P("serve", "head", None, None, None),
            P("serve", "head", None, None, None),
            P(),
            P(),
            P(),
        ),
        out_specs=P(None, ("serve", "head"), None),
        check_vma=False,
    )
```

```python
import functools

import jax
import jax.numpy as jnp
from jax import lax
from jax.experimental import pallas as pl
from jax.experimental.pallas import tpu as pltpu
from jax.sharding import PartitionSpec as P

NZ = 16
G = 8
MESH = pl.DeviceIdType.MESH
F32 = jnp.float32
BF16 = jnp.bfloat16
LOG2E = 1.4426950408889634


def dot(a, b, dims):
    return lax.dot_general(a, b, (dims, ((), ())), preferred_element_type=F32)


def wait_bytes(ref, sem):
    pltpu.make_async_copy(ref, ref, sem).wait()


def kernel(
    cfg,
    q_hbm, fresh_hbm, slot_hbm, len_hbm, owner_hbm, suffix_hbm, prefix_hbm,
    out_ref,
    q_ref, fresh_ref, slot_ref, len_ref, owner_ref, suffix, prefix,
    stage, hsend, hin, fsend, fin, table_v, table_s,
    qsend, qin, osend, oin, lflat, lsend, lin,
    own_out, own_lse, scores, asend, ain,
    load_sem, table_sem, head_sem, fresh_sem, out_sem,
    qrecv_sem, qsend_sem, osend_sem, lse_sem,
):
    steps, per, heads, ny, nz, prompts = cfg
    serve = ny * nz
    host = per * heads
    hd = 128
    rows = steps * G
    far = nz // 2
    me_s = lax.axis_index("serve")
    me_h = lax.axis_index("head")
    my_y, my_z = me_s // nz, me_s % nz
    scale = hd**-0.5

    def at(y, z):
        return ((my_y + y) & (ny - 1)) * nz + ((my_z + z) & (nz - 1))

    mine = serve - ny

    def distance(n):
        i = n // ny
        if isinstance(n, int):
            return n % ny, far - (i + 1) // 2 if i % 2 == 1 else far + i // 2
        return n % ny, jnp.where(i % 2 == 1, far - (i + 1) // 2, far + i // 2)

    def ahead(n):
        return at(*distance(n))

    def behind(n):
        y, z = distance(n)
        return at(-y, -z)

    def send(src, dst, send_sem, recv_sem, s, h):
        pltpu.make_async_remote_copy(
            src_ref=src,
            dst_ref=dst,
            send_sem=send_sem,
            recv_sem=recv_sem,
            device_id=(s, h),
            device_id_type=MESH,
        ).start()

    def fori(low, high, body):
        def step(i, _):
            body(i)
            return 0

        lax.fori_loop(low, high, step, 0)

    loads = [
        pltpu.make_async_copy(src, dst, load_sem.at[i])
        for i, (src, dst) in enumerate(
            (
                (q_hbm, q_ref),
                (fresh_hbm, fresh_ref),
                (slot_hbm, slot_ref),
                (len_hbm, len_ref),
                (owner_hbm, owner_ref),
                (prefix_hbm, prefix),
                (suffix_hbm, suffix),
            )
        )
    ]
    for load in loads:
        load.start()

    barrier = pltpu.get_barrier_semaphore()

    def greet(s, h):
        pl.semaphore_signal(barrier, inc=1, device_id=(s, h), device_id_type=MESH)

    for n in range(serve):
        if n != mine:
            greet(ahead(n), me_h)
    for i in range(1, heads):
        greet(me_s, (me_h + i) & (heads - 1))

    loads[0].wait()
    for t in range(steps):
        wide = q_ref[t].astype(F32)
        for c in range(heads):
            for g in range(G):
                col = (c * G + g) * hd
                stage[c, pl.ds(t * G + g, per, stride=rows), :] = wide[:, col : col + hd]
    for c in range(heads):
        hsend[c] = stage[c].astype(BF16).reshape(per, rows, hd)
    used = per * steps
    loads[1].wait()
    for t in range(steps):
        wide = fresh_ref[t].astype(F32)
        for c in range(heads):
            for kv in range(2):
                col = (2 * c + kv) * hd
                stage[c, pl.ds(kv * rows + t, per, stride=steps), :] = wide[:, col : col + hd]
    for c in range(heads):
        for kv in range(2):
            stage[c, kv * rows + used : (kv + 1) * rows, :] = jnp.zeros((rows - used, hd), F32)
        fsend[c] = stage[c, 0 : 2 * rows, :].astype(BF16).reshape(2, rows, hd)

    for i in (2, 3, 4):
        loads[i].wait()
    lane = lax.broadcasted_iota(jnp.int32, (host, 128), 1)
    sub = lax.broadcasted_iota(jnp.int32, (host, 128), 0)
    wanted = sub + me_s * host
    found = jnp.zeros((host, 128), jnp.int32)
    for r in range(slot_ref.shape[0]):
        here = jnp.broadcast_to(slot_ref[r : r + 1, :], (host, 128)) == wanted
        held = (r * 128 + lane) // serve * 256 + jnp.broadcast_to(len_ref[r : r + 1, :], (host, 128))
        found = found + jnp.where(here, held, 0)
    found = jnp.broadcast_to(jnp.sum(found, axis=1, keepdims=True), (host, 128))
    prompt_of = found >> 8
    places, sent = [], sub * 0
    for i in range(2):
        half = sub * 0
        for p in range(prompts):
            half = jnp.where(prompt_of == p, owner_ref[i, p], half)
        sent = jnp.where(half == lane, sub, sent)
        y = ((half >> 1) // nz - my_y) & (ny - 1)
        z = ((half >> 1) - my_z) & (nz - 1)
        i = jnp.where(z < far, 2 * (far - z) - 1, 2 * (z - far))
        places.append((i * ny + y) * 2 + (half & 1))
    table_v[0:host, :] = jnp.where(
        lane == 0, places[0], jnp.where(lane == 1, places[1], found & 255)
    )
    table_v[host : host + 8, :] = jnp.broadcast_to(jnp.max(sent, axis=0, keepdims=True), (8, 128))
    table_copy = pltpu.make_async_copy(table_v, table_s, table_sem)
    table_copy.start()

    pl.semaphore_wait(barrier, serve - 1 + heads - 1)

    def send_head(i):
        c = (me_h + i) & (heads - 1)
        send(hsend.at[c], hin.at[me_h], head_sem.at[0], head_sem.at[1], me_s, c)

    def send_fresh(i):
        c = (me_h + i) & (heads - 1)
        send(fsend.at[c], fin.at[me_h], fresh_sem.at[0], fresh_sem.at[1], me_s, c)

    fori(1, heads, send_head)
    fori(1, heads, send_fresh)
    hin[me_h] = hsend[me_h]
    fin[me_h] = fsend[me_h]
    table_copy.wait()
    wait_bytes(hin.at[pl.ds(0, heads - 1)], head_sem.at[1])

    def pick(d, j):
        k = table_s[host, d * 2 + j]
        return hin[k // per, k % per]

    def gather(shift, d):
        for j in range(2):
            qsend[shift, j] = pick(d, j)

    def send_queries(n):
        d = ahead(n)
        gather(n, d)
        send(qsend.at[n], qin.at[n], qsend_sem, qrecv_sem.at[n // nz], d, me_h)

    fori(0, mine, send_queries)
    fori(mine + 1, serve, send_queries)
    gather(mine, me_s)
    qin[mine] = qsend[mine]

    loads[6].wait()
    lanes16 = lax.broadcasted_iota(jnp.int32, (rows, 128), 1)
    sub16 = lax.broadcasted_iota(jnp.int32, (rows, 128), 0)

    def own_scores(c):
        for i in range(per):
            k = c * per + i
            s = dot(hin[c, i], suffix[k, 0], ((1,), (1,)))
            scores[k] = jnp.where(lanes16 < table_s[k, 2], s, -jnp.inf)

    fori(0, heads, own_scores)
    wait_bytes(fin.at[pl.ds(0, heads - 1)], fresh_sem.at[1])
    col = lax.broadcasted_iota(jnp.int32, (host * rows, heads * rows), 1)
    row = lax.broadcasted_iota(jnp.int32, (host * rows, heads * rows), 0)
    col_sample = col // rows * per + col % rows // steps
    live = (
        (col_sample == row // rows) & (col % rows < used) & (col % steps <= row % rows // G)
    )
    q_all = hin[...].reshape(host * rows, hd)
    fresh_k = fin[:, 0].reshape(heads * rows, hd)
    fresh_v = fin[:, 1].reshape(heads * rows, hd)
    fresh_scores = jnp.where(live, dot(q_all, fresh_k, ((1,), (1,))), -jnp.inf)
    cache_scores = scores[...].reshape(host * rows, 128)
    top = jnp.maximum(
        jnp.max(cache_scores, axis=1, keepdims=True), jnp.max(fresh_scores, axis=1, keepdims=True)
    )
    cache_exp = jnp.exp((cache_scores - top) * scale)
    fresh_exp = jnp.exp((fresh_scores - top) * scale)
    total = jnp.sum(cache_exp, axis=1, keepdims=True) + jnp.sum(fresh_exp, axis=1, keepdims=True)
    scores[...] = cache_exp.reshape(host, rows, 128)
    own_out[...] = dot(fresh_exp.astype(BF16), fresh_v, ((1,), (0,))).reshape(host, rows, hd)
    own_lse[...] = jnp.broadcast_to(top * scale + jnp.log(total), (host * rows, 128)).reshape(
        host, rows, 128
    )
    inverse = jnp.broadcast_to(1.0 / total, (host * rows, 128)).reshape(host, rows, 128)

    def own_values(c):
        for i in range(per):
            k = c * per + i
            own_out[k] = own_out[k] + dot(scores[k].astype(BF16), suffix[k, 1], ((1,), (0,)))

    fori(0, heads, own_values)
    own_out[...] = own_out[...] * inverse

    loads[5].wait()
    tile = nz * rows

    def group(r):
        @pl.when(r == ny - 1)
        def _():
            wait_bytes(qin.at[pl.ds(0, nz - 1)], qrecv_sem.at[ny - 1])

        @pl.when(r < ny - 1)
        def _():
            wait_bytes(qin.at[pl.ds(0, nz)], qrecv_sem.at[r])

        first = r * nz

        def half(j):
            q = qin[pl.ds(first, nz), j].reshape(tile, hd)
            s = dot(q, prefix[j, 0], ((1,), (1,)))
            top = jnp.max(s, axis=1, keepdims=True)
            p = jnp.exp2(s * (scale * LOG2E) - top * (scale * LOG2E))
            total = jnp.sum(p, axis=1, keepdims=True)
            o = dot(p.astype(BF16), prefix[j, 1], ((1,), (0,))) / total
            osend[pl.ds(first, nz), j] = o.astype(BF16).reshape(nz, rows, hd)
            lse = jnp.broadcast_to(top * scale + jnp.log(total), (tile, 128))
            for b in range(tile // 128):
                lflat[j, b : b + 1, :] = jnp.transpose(lse[b * 128 : (b + 1) * 128, :])[0:1, :]

        fori(0, 2, half)
        low = lax.broadcasted_iota(jnp.int32, (1, 128), 1) < 64
        for b in range(tile // 128):
            line0, line1 = lflat[0, b : b + 1, :], lflat[1, b : b + 1, :]
            place = r * (nz // 4) + b * 2
            lsend[place] = jnp.where(low, line0, pltpu.roll(line1, 64, 1))
            lsend[place + 1] = jnp.where(low, pltpu.roll(line0, 64, 1), line1)

        def send_lse(n):
            send(lsend.at[n // 4], lin.at[n], lse_sem.at[0], lse_sem.at[1], behind(n), me_h)

        def send_back(n):
            send(osend.at[n], oin.at[n], osend_sem.at[0], osend_sem.at[1], behind(n), me_h)

        stop = jnp.where(r == ny - 1, mine, first + nz)
        fori(first, stop, send_lse)
        fori(first, stop, send_back)

        @pl.when(r == ny - 1)
        def _():
            fori(mine + 1, serve, send_lse)
            fori(mine + 1, serve, send_back)

    fori(0, ny, group)
    oin[mine] = osend[mine]
    lin[mine] = lsend[mine // 4]
    wait_bytes(lin.at[pl.ds(0, serve - 1)], lse_sem.at[1])

    def weigh(c):
        for m in range(per):
            k = c * per + m
            logs = []
            for i in range(2):
                place = table_s[k, i]
                n = place >> 1
                line = jnp.broadcast_to(lin[n], (rows, 128))
                here = lanes16 == sub16 + (n & 3) * rows + (place & 1) * 64
                logs.append(jnp.sum(jnp.where(here, line, 0.0), axis=1, keepdims=True))
            own = own_lse[k]
            top = jnp.maximum(jnp.maximum(logs[0], logs[1]), own)
            a0, a1, a2 = jnp.exp(logs[0] - top), jnp.exp(logs[1] - top), jnp.exp(own - top)
            inverse = 1.0 / (a0 + a1 + a2)
            scores[k] = a0 * inverse
            own_lse[k] = a1 * inverse
            own_out[k] = own_out[k] * (a2 * inverse)

    fori(0, heads, weigh)
    wait_bytes(oin.at[pl.ds(0, serve - 1)], osend_sem.at[1])

    def mix(c, dst):
        for n in range(per):
            k = c * per + n
            p0, p1 = table_s[k, 0], table_s[k, 1]
            half0 = oin[p0 >> 1, p0 & 1].astype(F32)
            half1 = oin[p1 >> 1, p1 & 1].astype(F32)
            dst[c, n] = (scores[k] * half0 + own_lse[k] * half1 + own_out[k]).astype(BF16)

    def send_out(i):
        c = (me_h + i) & (heads - 1)
        mix(c, asend)
        send(asend.at[c], ain.at[me_h], out_sem.at[0], out_sem.at[1], me_s, c)

    fori(1, heads, send_out)
    mix(me_h, ain)
    wait_bytes(ain.at[pl.ds(0, heads - 1)], out_sem.at[1])
    for c in range(heads):
        stage[c] = ain[c].astype(F32).reshape(per * rows, hd)
    for t in range(steps):
        for c in range(heads):
            for g in range(G):
                col = (c * G + g) * hd
                out_ref[t, :, col : col + hd] = stage[
                    c, pl.ds(t * G + g, per, stride=rows), :
                ].astype(BF16)

    wait_bytes(qsend.at[pl.ds(0, serve - 1)], qsend_sem)
    wait_bytes(osend.at[pl.ds(0, serve - 1)], osend_sem.at[0])
    wait_bytes(lin.at[pl.ds(0, serve - 1)], lse_sem.at[0])
    wait_bytes(hsend.at[pl.ds(0, heads - 1)], head_sem.at[0])
    wait_bytes(fsend.at[pl.ds(0, heads - 1)], fresh_sem.at[0])
    wait_bytes(asend.at[pl.ds(0, heads - 1)], out_sem.at[0])


def local(queries, new_kv, suffix_kv, prefix_kv, owner_map, host_slot, suffix_len):
    serve, heads = lax.axis_size("serve"), lax.axis_size("head")
    steps, per = queries.shape[0], queries.shape[1]
    host, slab = suffix_kv.shape[0], prefix_kv.shape[3]
    prompts, samples = owner_map.shape[0], host_slot.shape[0]
    nz = NZ
    ny = serve // nz
    rows, hd = steps * G, 128
    cfg = (steps, per, heads, ny, nz, prompts)
    dma = pltpu.SemaphoreType.DMA
    hbm = pl.BlockSpec(memory_space=pltpu.HBM)
    return pl.pallas_call(
        functools.partial(kernel, cfg),
        out_shape=pltpu.VMEM(queries.shape, BF16),
        in_specs=[hbm] * 7,
        out_specs=pl.BlockSpec(memory_space=pltpu.VMEM),
        scratch_shapes=[
            pltpu.VMEM(queries.shape, BF16),
            pltpu.VMEM(new_kv.shape, BF16),
            pltpu.VMEM((samples // 128, 128), jnp.int32),
            pltpu.VMEM((samples // 128, 128), jnp.int32),
            pltpu.SMEM((2, prompts), jnp.int32),
            pltpu.VMEM((host, 2, 128, hd), BF16),
            pltpu.VMEM((2, 2, slab, hd), BF16),
            pltpu.VMEM((heads, per * rows, hd), F32),
            pltpu.VMEM((heads, per, rows, hd), BF16),
            pltpu.VMEM((heads, per, rows, hd), BF16),
            pltpu.VMEM((heads, 2, rows, hd), BF16),
            pltpu.VMEM((heads, 2, rows, hd), BF16),
            pltpu.VMEM((host + 8, 128), jnp.int32),
            pltpu.SMEM((host + 8, 128), jnp.int32),
            pltpu.VMEM((serve, 2, rows, hd), BF16),
            pltpu.VMEM((serve, 2, rows, hd), BF16),
            pltpu.VMEM((serve, 2, rows, hd), BF16),
            pltpu.VMEM((serve, 2, rows, hd), BF16),
            pltpu.VMEM((2, 8, 128), F32),
            pltpu.VMEM((serve // 4, 1, 128), F32),
            pltpu.VMEM((serve, 1, 128), F32),
            pltpu.VMEM((host, rows, hd), F32),
            pltpu.VMEM((host, rows, 128), F32),
            pltpu.VMEM((host, rows, 128), F32),
            pltpu.VMEM((heads, per, rows, hd), BF16),
            pltpu.VMEM((heads, per, rows, hd), BF16),
            dma((7,)),
            dma,
            dma((2,)),
            dma((2,)),
            dma((2,)),
            dma((ny,)),
            dma,
            dma((2,)),
            dma((2,)),
        ],
        compiler_params=pltpu.CompilerParams(
            collective_id=0, has_side_effects=True, vmem_limit_bytes=57 * 1024 * 1024
        ),
    )(
        queries,
        new_kv,
        host_slot.reshape(-1, 128),
        suffix_len.reshape(-1, 128),
        owner_map.T,
        suffix_kv.reshape(host, 2, 128, hd),
        prefix_kv.reshape(2, 2, slab, hd),
    )


def solution(mesh):
    return jax.shard_map(
        local,
        mesh=mesh,
        in_specs=(
            P(None, ("serve", "head"), None),
            P(None, ("serve", "head"), None),
            P("serve", "head", None, None, None),
            P("serve", "head", None, None, None),
            P(),
            P(),
            P(),
        ),
        out_specs=P(None, ("serve", "head"), None),
        check_vma=False,
    )
```

```python
import functools

import jax
import jax.numpy as jnp
from jax import lax
from jax.experimental import pallas as pl
from jax.experimental.pallas import tpu as pltpu
from jax.sharding import PartitionSpec as P

NZ = 16
G = 8
MESH = pl.DeviceIdType.MESH
F32 = jnp.float32
BF16 = jnp.bfloat16
LOG2E = 1.4426950408889634


def dot(a, b, dims):
    return lax.dot_general(a, b, (dims, ((), ())), preferred_element_type=F32)


def wait_bytes(ref, sem):
    pltpu.make_async_copy(ref, ref, sem).wait()


def kernel(
    cfg,
    q_hbm, fresh_hbm, slot_hbm, len_hbm, owner_hbm, suffix_hbm, prefix_hbm,
    out_ref,
    q_ref, fresh_ref, slot_ref, len_ref, owner_ref, suffix, prefix,
    stage, hsend, hin, fsend, fin, table_v, table_s,
    qsend, qin, osend, oin, lflat, lsend, lin,
    own_out, own_lse, scores, asend, ain,
    load_sem, table_sem, head_sem, fresh_sem, out_sem,
    qrecv_sem, qsend_sem, osend_sem, lse_sem,
):
    steps, per, heads, ny, nz, prompts = cfg
    serve = ny * nz
    host = per * heads
    hd = 128
    rows = steps * G
    far = nz // 2
    me_s = lax.axis_index("serve")
    me_h = lax.axis_index("head")
    my_y, my_z = me_s // nz, me_s % nz
    scale = hd**-0.5

    def at(y, z):
        return ((my_y + y) & (ny - 1)) * nz + ((my_z + z) & (nz - 1))

    mine = nz - 1

    def distance(n):
        i = n % nz
        if isinstance(n, int):
            return n // nz, far - (i + 1) // 2 if i % 2 == 1 else far + i // 2
        return n // nz, jnp.where(i % 2 == 1, far - (i + 1) // 2, far + i // 2)

    def ahead(n):
        return at(*distance(n))

    def behind(n):
        y, z = distance(n)
        return at(-y, -z)

    def send(src, dst, send_sem, recv_sem, s, h):
        pltpu.make_async_remote_copy(
            src_ref=src,
            dst_ref=dst,
            send_sem=send_sem,
            recv_sem=recv_sem,
            device_id=(s, h),
            device_id_type=MESH,
        ).start()

    def fori(low, high, body):
        def step(i, _):
            body(i)
            return 0

        lax.fori_loop(low, high, step, 0)

    loads = [
        pltpu.make_async_copy(src, dst, load_sem.at[i])
        for i, (src, dst) in enumerate(
            (
                (q_hbm, q_ref),
                (fresh_hbm, fresh_ref),
                (slot_hbm, slot_ref),
                (len_hbm, len_ref),
                (owner_hbm, owner_ref),
                (prefix_hbm, prefix),
                (suffix_hbm, suffix),
            )
        )
    ]
    for load in loads:
        load.start()

    barrier = pltpu.get_barrier_semaphore()

    def greet(s, h):
        pl.semaphore_signal(barrier, inc=1, device_id=(s, h), device_id_type=MESH)

    for n in range(serve):
        if n != mine:
            greet(ahead(n), me_h)
    for i in range(1, heads):
        greet(me_s, (me_h + i) & (heads - 1))

    loads[0].wait()
    for t in range(steps):
        wide = q_ref[t].astype(F32)
        for c in range(heads):
            for g in range(G):
                col = (c * G + g) * hd
                stage[c, pl.ds(t * G + g, per, stride=rows), :] = wide[:, col : col + hd]
    for c in range(heads):
        hsend[c] = stage[c].astype(BF16).reshape(per, rows, hd)
    used = per * steps
    loads[1].wait()
    for t in range(steps):
        wide = fresh_ref[t].astype(F32)
        for c in range(heads):
            for kv in range(2):
                col = (2 * c + kv) * hd
                stage[c, pl.ds(kv * rows + t, per, stride=steps), :] = wide[:, col : col + hd]
    for c in range(heads):
        for kv in range(2):
            stage[c, kv * rows + used : (kv + 1) * rows, :] = jnp.zeros((rows - used, hd), F32)
        fsend[c] = stage[c, 0 : 2 * rows, :].astype(BF16).reshape(2, rows, hd)

    for i in (2, 3, 4):
        loads[i].wait()
    lane = lax.broadcasted_iota(jnp.int32, (host, 128), 1)
    sub = lax.broadcasted_iota(jnp.int32, (host, 128), 0)
    wanted = sub + me_s * host
    found = jnp.zeros((host, 128), jnp.int32)
    for r in range(slot_ref.shape[0]):
        here = jnp.broadcast_to(slot_ref[r : r + 1, :], (host, 128)) == wanted
        held = (r * 128 + lane) // serve * 256 + jnp.broadcast_to(len_ref[r : r + 1, :], (host, 128))
        found = found + jnp.where(here, held, 0)
    found = jnp.broadcast_to(jnp.sum(found, axis=1, keepdims=True), (host, 128))
    prompt_of = found >> 8
    places, sent = [], sub * 0
    for i in range(2):
        half = sub * 0
        for p in range(prompts):
            half = jnp.where(prompt_of == p, owner_ref[i, p], half)
        sent = jnp.where(half == lane, sub, sent)
        y = ((half >> 1) // nz - my_y) & (ny - 1)
        z = ((half >> 1) - my_z) & (nz - 1)
        i = jnp.where(z < far, 2 * (far - z) - 1, 2 * (z - far))
        places.append((y * nz + i) * 2 + (half & 1))
    table_v[0:host, :] = jnp.where(
        lane == 0, places[0], jnp.where(lane == 1, places[1], found & 255)
    )
    table_v[host : host + 8, :] = jnp.broadcast_to(jnp.max(sent, axis=0, keepdims=True), (8, 128))
    table_copy = pltpu.make_async_copy(table_v, table_s, table_sem)
    table_copy.start()

    pl.semaphore_wait(barrier, serve - 1 + heads - 1)

    def send_head(i):
        c = (me_h + i) & (heads - 1)
        send(hsend.at[c], hin.at[me_h], head_sem.at[0], head_sem.at[1], me_s, c)

    def send_fresh(i):
        c = (me_h + i) & (heads - 1)
        send(fsend.at[c], fin.at[me_h], fresh_sem.at[0], fresh_sem.at[1], me_s, c)

    fori(1, heads, send_head)
    fori(1, heads, send_fresh)
    hin[me_h] = hsend[me_h]
    fin[me_h] = fsend[me_h]
    table_copy.wait()
    wait_bytes(hin.at[pl.ds(0, heads - 1)], head_sem.at[1])

    def pick(d, j):
        k = table_s[host, d * 2 + j]
        return hin[k // per, k % per]

    def gather(shift, d):
        for j in range(2):
            qsend[shift, j] = pick(d, j)

    def send_queries(n):
        d = ahead(n)
        gather(n, d)
        send(qsend.at[n], qin.at[n], qsend_sem, qrecv_sem.at[n // nz], d, me_h)

    fori(0, mine, send_queries)
    fori(mine + 1, serve, send_queries)
    gather(mine, me_s)
    qin[mine] = qsend[mine]

    loads[6].wait()
    lanes16 = lax.broadcasted_iota(jnp.int32, (rows, 128), 1)
    sub16 = lax.broadcasted_iota(jnp.int32, (rows, 128), 0)

    def own_scores(c):
        for i in range(per):
            k = c * per + i
            s = dot(hin[c, i], suffix[k, 0], ((1,), (1,)))
            scores[k] = jnp.where(lanes16 < table_s[k, 2], s, -jnp.inf)

    fori(0, heads, own_scores)
    wait_bytes(fin.at[pl.ds(0, heads - 1)], fresh_sem.at[1])
    col = lax.broadcasted_iota(jnp.int32, (host * rows, heads * rows), 1)
    row = lax.broadcasted_iota(jnp.int32, (host * rows, heads * rows), 0)
    col_sample = col // rows * per + col % rows // steps
    live = (
        (col_sample == row // rows) & (col % rows < used) & (col % steps <= row % rows // G)
    )
    q_all = hin[...].reshape(host * rows, hd)
    fresh_k = fin[:, 0].reshape(heads * rows, hd)
    fresh_v = fin[:, 1].reshape(heads * rows, hd)
    fresh_scores = jnp.where(live, dot(q_all, fresh_k, ((1,), (1,))), -jnp.inf)
    cache_scores = scores[...].reshape(host * rows, 128)
    top = jnp.maximum(
        jnp.max(cache_scores, axis=1, keepdims=True), jnp.max(fresh_scores, axis=1, keepdims=True)
    )
    cache_exp = jnp.exp((cache_scores - top) * scale)
    fresh_exp = jnp.exp((fresh_scores - top) * scale)
    total = jnp.sum(cache_exp, axis=1, keepdims=True) + jnp.sum(fresh_exp, axis=1, keepdims=True)
    scores[...] = cache_exp.reshape(host, rows, 128)
    own_out[...] = dot(fresh_exp.astype(BF16), fresh_v, ((1,), (0,))).reshape(host, rows, hd)
    own_lse[...] = jnp.broadcast_to(top * scale + jnp.log(total), (host * rows, 128)).reshape(
        host, rows, 128
    )
    inverse = jnp.broadcast_to(1.0 / total, (host * rows, 128)).reshape(host, rows, 128)

    def own_values(c):
        for i in range(per):
            k = c * per + i
            own_out[k] = own_out[k] + dot(scores[k].astype(BF16), suffix[k, 1], ((1,), (0,)))

    fori(0, heads, own_values)
    own_out[...] = own_out[...] * inverse

    loads[5].wait()
    tile = nz * rows

    def group(r):
        @pl.when(r == 0)
        def _():
            wait_bytes(qin.at[pl.ds(0, nz - 1)], qrecv_sem.at[0])

        @pl.when(r > 0)
        def _():
            wait_bytes(qin.at[pl.ds(0, nz)], qrecv_sem.at[r])

        first = r * nz

        def half(j):
            q = qin[pl.ds(first, nz), j].reshape(tile, hd)
            s = dot(q, prefix[j, 0], ((1,), (1,)))
            top = jnp.max(s, axis=1, keepdims=True)
            p = jnp.exp2(s * (scale * LOG2E) - top * (scale * LOG2E))
            total = jnp.sum(p, axis=1, keepdims=True)
            o = dot(p.astype(BF16), prefix[j, 1], ((1,), (0,))) / total
            osend[pl.ds(first, nz), j] = o.astype(BF16).reshape(nz, rows, hd)
            lse = jnp.broadcast_to(top * scale + jnp.log(total), (tile, 128))
            for b in range(tile // 128):
                lflat[j, b : b + 1, :] = jnp.transpose(lse[b * 128 : (b + 1) * 128, :])[0:1, :]

        fori(0, 2, half)
        low = lax.broadcasted_iota(jnp.int32, (1, 128), 1) < 64
        for b in range(tile // 128):
            line0, line1 = lflat[0, b : b + 1, :], lflat[1, b : b + 1, :]
            place = r * (nz // 4) + b * 2
            lsend[place] = jnp.where(low, line0, pltpu.roll(line1, 64, 1))
            lsend[place + 1] = jnp.where(low, pltpu.roll(line0, 64, 1), line1)

        def send_lse(n):
            send(lsend.at[n // 4], lin.at[n], lse_sem.at[0], lse_sem.at[1], behind(n), me_h)

        def send_back(n):
            send(osend.at[n], oin.at[n], osend_sem.at[0], osend_sem.at[1], behind(n), me_h)

        def lse_other(n):
            @pl.when(n != mine)
            def _():
                send_lse(n)

        def send_some(q, k):
            def one(n):
                z = (my_z - distance(n)[1]) & (nz - 1)
                quarter = jnp.minimum(z // (nz // 4), 2)

                @pl.when((quarter == k) & (n != mine))
                def _():
                    send_back(n)

            fori(q * nz, q * nz + nz, one)

        fori(first, first + nz, lse_other)
        for k in range(3):

            @pl.when(r >= k)
            def _(k=k):
                send_some(r - k, k)

        @pl.when(r == ny - 1)
        def _():
            for k in range(3):
                fori(ny - k, ny, lambda q, k=k: send_some(q, k))

    fori(0, ny, group)
    oin[mine] = osend[mine]
    lin[mine] = lsend[mine // 4]
    wait_bytes(lin.at[pl.ds(0, serve - 1)], lse_sem.at[1])

    def weigh(c):
        for m in range(per):
            k = c * per + m
            logs = []
            for i in range(2):
                place = table_s[k, i]
                n = place >> 1
                line = jnp.broadcast_to(lin[n], (rows, 128))
                here = lanes16 == sub16 + (n & 3) * rows + (place & 1) * 64
                logs.append(jnp.sum(jnp.where(here, line, 0.0), axis=1, keepdims=True))
            own = own_lse[k]
            top = jnp.maximum(jnp.maximum(logs[0], logs[1]), own)
            a0, a1, a2 = jnp.exp(logs[0] - top), jnp.exp(logs[1] - top), jnp.exp(own - top)
            inverse = 1.0 / (a0 + a1 + a2)
            scores[k] = a0 * inverse
            own_lse[k] = a1 * inverse
            own_out[k] = own_out[k] * (a2 * inverse)

    fori(0, heads, weigh)
    wait_bytes(oin.at[pl.ds(0, serve - 1)], osend_sem.at[1])

    def mix(c, dst):
        for n in range(per):
            k = c * per + n
            p0, p1 = table_s[k, 0], table_s[k, 1]
            half0 = oin[p0 >> 1, p0 & 1].astype(F32)
            half1 = oin[p1 >> 1, p1 & 1].astype(F32)
            dst[c, n] = (scores[k] * half0 + own_lse[k] * half1 + own_out[k]).astype(BF16)

    def send_out(i):
        c = (me_h + i) & (heads - 1)
        mix(c, asend)
        send(asend.at[c], ain.at[me_h], out_sem.at[0], out_sem.at[1], me_s, c)

    fori(1, heads, send_out)
    mix(me_h, ain)
    wait_bytes(ain.at[pl.ds(0, heads - 1)], out_sem.at[1])
    for c in range(heads):
        stage[c] = ain[c].astype(F32).reshape(per * rows, hd)
    for t in range(steps):
        for c in range(heads):
            for g in range(G):
                col = (c * G + g) * hd
                out_ref[t, :, col : col + hd] = stage[
                    c, pl.ds(t * G + g, per, stride=rows), :
                ].astype(BF16)

    wait_bytes(qsend.at[pl.ds(0, serve - 1)], qsend_sem)
    wait_bytes(osend.at[pl.ds(0, serve - 1)], osend_sem.at[0])
    wait_bytes(lin.at[pl.ds(0, serve - 1)], lse_sem.at[0])
    wait_bytes(hsend.at[pl.ds(0, heads - 1)], head_sem.at[0])
    wait_bytes(fsend.at[pl.ds(0, heads - 1)], fresh_sem.at[0])
    wait_bytes(asend.at[pl.ds(0, heads - 1)], out_sem.at[0])


def local(queries, new_kv, suffix_kv, prefix_kv, owner_map, host_slot, suffix_len):
    serve, heads = lax.axis_size("serve"), lax.axis_size("head")
    steps, per = queries.shape[0], queries.shape[1]
    host, slab = suffix_kv.shape[0], prefix_kv.shape[3]
    prompts, samples = owner_map.shape[0], host_slot.shape[0]
    nz = NZ
    ny = serve // nz
    rows, hd = steps * G, 128
    cfg = (steps, per, heads, ny, nz, prompts)
    dma = pltpu.SemaphoreType.DMA
    hbm = pl.BlockSpec(memory_space=pltpu.HBM)
    return pl.pallas_call(
        functools.partial(kernel, cfg),
        out_shape=pltpu.VMEM(queries.shape, BF16),
        in_specs=[hbm] * 7,
        out_specs=pl.BlockSpec(memory_space=pltpu.VMEM),
        scratch_shapes=[
            pltpu.VMEM(queries.shape, BF16),
            pltpu.VMEM(new_kv.shape, BF16),
            pltpu.VMEM((samples // 128, 128), jnp.int32),
            pltpu.VMEM((samples // 128, 128), jnp.int32),
            pltpu.SMEM((2, prompts), jnp.int32),
            pltpu.VMEM((host, 2, 128, hd), BF16),
            pltpu.VMEM((2, 2, slab, hd), BF16),
            pltpu.VMEM((heads, per * rows, hd), F32),
            pltpu.VMEM((heads, per, rows, hd), BF16),
            pltpu.VMEM((heads, per, rows, hd), BF16),
            pltpu.VMEM((heads, 2, rows, hd), BF16),
            pltpu.VMEM((heads, 2, rows, hd), BF16),
            pltpu.VMEM((host + 8, 128), jnp.int32),
            pltpu.SMEM((host + 8, 128), jnp.int32),
            pltpu.VMEM((serve, 2, rows, hd), BF16),
            pltpu.VMEM((serve, 2, rows, hd), BF16),
            pltpu.VMEM((serve, 2, rows, hd), BF16),
            pltpu.VMEM((serve, 2, rows, hd), BF16),
            pltpu.VMEM((2, 8, 128), F32),
            pltpu.VMEM((serve // 4, 1, 128), F32),
            pltpu.VMEM((serve, 1, 128), F32),
            pltpu.VMEM((host, rows, hd), F32),
            pltpu.VMEM((host, rows, 128), F32),
            pltpu.VMEM((host, rows, 128), F32),
            pltpu.VMEM((heads, per, rows, hd), BF16),
            pltpu.VMEM((heads, per, rows, hd), BF16),
            dma((7,)),
            dma,
            dma((2,)),
            dma((2,)),
            dma((2,)),
            dma((ny,)),
            dma,
            dma((2,)),
            dma((2,)),
        ],
        compiler_params=pltpu.CompilerParams(
            collective_id=0, has_side_effects=True, vmem_limit_bytes=57 * 1024 * 1024
        ),
    )(
        queries,
        new_kv,
        host_slot.reshape(-1, 128),
        suffix_len.reshape(-1, 128),
        owner_map.T,
        suffix_kv.reshape(host, 2, 128, hd),
        prefix_kv.reshape(2, 2, slab, hd),
    )


def solution(mesh):
    return jax.shard_map(
        local,
        mesh=mesh,
        in_specs=(
            P(None, ("serve", "head"), None),
            P(None, ("serve", "head"), None),
            P("serve", "head", None, None, None),
            P("serve", "head", None, None, None),
            P(),
            P(),
            P(),
        ),
        out_specs=P(None, ("serve", "head"), None),
        check_vma=False,
    )
```

```python
import functools

import jax
import jax.numpy as jnp
from jax import lax
from jax.experimental import pallas as pl
from jax.experimental.pallas import tpu as pltpu
from jax.sharding import PartitionSpec as P

NZ = 16
G = 8
MESH = pl.DeviceIdType.MESH
F32 = jnp.float32
BF16 = jnp.bfloat16
LOG2E = 1.4426950408889634


def dot(a, b, dims):
    return lax.dot_general(a, b, (dims, ((), ())), preferred_element_type=F32)


def wait_bytes(ref, sem):
    pltpu.make_async_copy(ref, ref, sem).wait()


def kernel(
    cfg,
    q_hbm, fresh_hbm, slot_hbm, len_hbm, owner_hbm, suffix_hbm, prefix_hbm,
    out_ref,
    q_ref, fresh_ref, slot_ref, len_ref, owner_ref, suffix, prefix,
    stage, hsend, hin, fsend, fin, table_v, table_s,
    qsend, qin, osend, oin, lflat, lsend, lin,
    own_out, own_lse, scores, asend, ain,
    load_sem, table_sem, head_sem, fresh_sem, out_sem,
    qrecv_sem, qsend_sem, osend_sem, lse_sem,
):
    steps, per, heads, ny, nz, prompts = cfg
    serve = ny * nz
    host = per * heads
    hd = 128
    rows = steps * G
    far = nz // 2
    me_s = lax.axis_index("serve")
    me_h = lax.axis_index("head")
    my_y, my_z = me_s // nz, me_s % nz
    scale = hd**-0.5

    def at(y, z):
        return ((my_y + y) & (ny - 1)) * nz + ((my_z + z) & (nz - 1))

    mine = nz - 1

    def distance(n):
        i = n % nz
        if isinstance(n, int):
            return n // nz, far - (i + 1) // 2 if i % 2 == 1 else far + i // 2
        return n // nz, jnp.where(i % 2 == 1, far - (i + 1) // 2, far + i // 2)

    def place_of(z):
        return jnp.where(z < far, 2 * (far - z) - 1, 2 * (z - far))

    def ahead(n):
        return at(*distance(n))

    def behind(n):
        y, z = distance(n)
        return at(-y, -z)

    def send(src, dst, send_sem, recv_sem, s, h):
        pltpu.make_async_remote_copy(
            src_ref=src,
            dst_ref=dst,
            send_sem=send_sem,
            recv_sem=recv_sem,
            device_id=(s, h),
            device_id_type=MESH,
        ).start()

    def fori(low, high, body):
        def step(i, _):
            body(i)
            return 0

        lax.fori_loop(low, high, step, 0)

    loads = [
        pltpu.make_async_copy(src, dst, load_sem.at[i])
        for i, (src, dst) in enumerate(
            (
                (q_hbm, q_ref),
                (fresh_hbm, fresh_ref),
                (slot_hbm, slot_ref),
                (len_hbm, len_ref),
                (owner_hbm, owner_ref),
                (prefix_hbm, prefix),
                (suffix_hbm, suffix),
            )
        )
    ]
    for load in loads:
        load.start()

    barrier = pltpu.get_barrier_semaphore()

    def greet(s, h):
        pl.semaphore_signal(barrier, inc=1, device_id=(s, h), device_id_type=MESH)

    def hops(n):
        y, z = distance(n)
        return min(y, ny - y) + min(z, nz - z)

    for n in sorted(range(serve), key=hops, reverse=True):
        if n != mine:
            greet(ahead(n), me_h)
    for i in range(1, heads):
        greet(me_s, (me_h + i) & (heads - 1))

    loads[0].wait()
    for t in range(steps):
        wide = q_ref[t].astype(F32)
        for c in range(heads):
            for g in range(G):
                col = (c * G + g) * hd
                stage[c, pl.ds(t * G + g, per, stride=rows), :] = wide[:, col : col + hd]
    for c in range(heads):
        hsend[c] = stage[c].astype(BF16).reshape(per, rows, hd)
    used = per * steps
    loads[1].wait()
    for t in range(steps):
        wide = fresh_ref[t].astype(F32)
        for c in range(heads):
            for kv in range(2):
                col = (2 * c + kv) * hd
                stage[c, pl.ds(kv * rows + t, per, stride=steps), :] = wide[:, col : col + hd]
    for c in range(heads):
        for kv in range(2):
            stage[c, kv * rows + used : (kv + 1) * rows, :] = jnp.zeros((rows - used, hd), F32)
        fsend[c] = stage[c, 0 : 2 * rows, :].astype(BF16).reshape(2, rows, hd)

    for i in (2, 3, 4):
        loads[i].wait()
    lane = lax.broadcasted_iota(jnp.int32, (host, 128), 1)
    sub = lax.broadcasted_iota(jnp.int32, (host, 128), 0)
    wanted = sub + me_s * host
    found = jnp.zeros((host, 128), jnp.int32)
    for r in range(slot_ref.shape[0]):
        here = jnp.broadcast_to(slot_ref[r : r + 1, :], (host, 128)) == wanted
        held = (r * 128 + lane) // serve * 256 + jnp.broadcast_to(len_ref[r : r + 1, :], (host, 128))
        found = found + jnp.where(here, held, 0)
    found = jnp.broadcast_to(jnp.sum(found, axis=1, keepdims=True), (host, 128))
    prompt_of = found >> 8
    places, sent = [], sub * 0
    for i in range(2):
        half = sub * 0
        for p in range(prompts):
            half = jnp.where(prompt_of == p, owner_ref[i, p], half)
        sent = jnp.where(half == lane, sub, sent)
        y = ((half >> 1) // nz - my_y) & (ny - 1)
        z = ((half >> 1) - my_z) & (nz - 1)
        places.append((y * nz + place_of(z)) * 2 + (half & 1))
    table_v[0:host, :] = jnp.where(
        lane == 0, places[0], jnp.where(lane == 1, places[1], found & 255)
    )
    table_v[host : host + 8, :] = jnp.broadcast_to(jnp.max(sent, axis=0, keepdims=True), (8, 128))
    table_copy = pltpu.make_async_copy(table_v, table_s, table_sem)
    table_copy.start()

    pl.semaphore_wait(barrier, serve - 1 + heads - 1)

    def send_head(i):
        c = (me_h + i) & (heads - 1)
        send(hsend.at[c], hin.at[me_h], head_sem.at[0], head_sem.at[1], me_s, c)

    def send_fresh(i):
        c = (me_h + i) & (heads - 1)
        send(fsend.at[c], fin.at[me_h], fresh_sem.at[0], fresh_sem.at[1], me_s, c)

    fori(1, heads, send_head)
    fori(1, heads, send_fresh)
    hin[me_h] = hsend[me_h]
    fin[me_h] = fsend[me_h]
    table_copy.wait()
    wait_bytes(hin.at[pl.ds(0, heads - 1)], head_sem.at[1])

    def pick(d, j):
        k = table_s[host, d * 2 + j]
        return hin[k // per, k % per]

    def gather(shift, d):
        for j in range(2):
            qsend[shift, j] = pick(d, j)

    def send_queries(n):
        d = ahead(n)
        gather(n, d)
        send(qsend.at[n], qin.at[n], qsend_sem, qrecv_sem.at[n // nz], d, me_h)

    fori(0, mine, send_queries)
    fori(mine + 1, serve, send_queries)
    gather(mine, me_s)
    qin[mine] = qsend[mine]

    loads[6].wait()
    lanes16 = lax.broadcasted_iota(jnp.int32, (rows, 128), 1)
    sub16 = lax.broadcasted_iota(jnp.int32, (rows, 128), 0)

    def own_scores(c):
        for i in range(per):
            k = c * per + i
            s = dot(hin[c, i], suffix[k, 0], ((1,), (1,)))
            scores[k] = jnp.where(lanes16 < table_s[k, 2], s, -jnp.inf)

    fori(0, heads, own_scores)
    wait_bytes(fin.at[pl.ds(0, heads - 1)], fresh_sem.at[1])
    col = lax.broadcasted_iota(jnp.int32, (host * rows, heads * rows), 1)
    row = lax.broadcasted_iota(jnp.int32, (host * rows, heads * rows), 0)
    col_sample = col // rows * per + col % rows // steps
    live = (
        (col_sample == row // rows) & (col % rows < used) & (col % steps <= row % rows // G)
    )
    q_all = hin[...].reshape(host * rows, hd)
    fresh_k = fin[:, 0].reshape(heads * rows, hd)
    fresh_v = fin[:, 1].reshape(heads * rows, hd)
    fresh_scores = jnp.where(live, dot(q_all, fresh_k, ((1,), (1,))), -jnp.inf)
    cache_scores = scores[...].reshape(host * rows, 128)
    top = jnp.maximum(
        jnp.max(cache_scores, axis=1, keepdims=True), jnp.max(fresh_scores, axis=1, keepdims=True)
    )
    cache_exp = jnp.exp((cache_scores - top) * scale)
    fresh_exp = jnp.exp((fresh_scores - top) * scale)
    total = jnp.sum(cache_exp, axis=1, keepdims=True) + jnp.sum(fresh_exp, axis=1, keepdims=True)
    scores[...] = cache_exp.reshape(host, rows, 128)
    own_out[...] = dot(fresh_exp.astype(BF16), fresh_v, ((1,), (0,))).reshape(host, rows, hd)
    own_lse[...] = jnp.broadcast_to(top * scale + jnp.log(total), (host * rows, 128)).reshape(
        host, rows, 128
    )
    inverse = jnp.broadcast_to(1.0 / total, (host * rows, 128)).reshape(host, rows, 128)

    def own_values(c):
        for i in range(per):
            k = c * per + i
            own_out[k] = own_out[k] + dot(scores[k].astype(BF16), suffix[k, 1], ((1,), (0,)))

    fori(0, heads, own_values)
    own_out[...] = own_out[...] * inverse

    loads[5].wait()
    tile = nz * rows

    def group(r):
        @pl.when(r == 0)
        def _():
            wait_bytes(qin.at[pl.ds(0, nz - 1)], qrecv_sem.at[0])

        @pl.when(r > 0)
        def _():
            wait_bytes(qin.at[pl.ds(0, nz)], qrecv_sem.at[r])

        first = r * nz

        def half(j):
            q = qin[pl.ds(first, nz), j].reshape(tile, hd)
            s = dot(q, prefix[j, 0], ((1,), (1,)))
            top = jnp.max(s, axis=1, keepdims=True)
            p = jnp.exp2(s * (scale * LOG2E) - top * (scale * LOG2E))
            total = jnp.sum(p, axis=1, keepdims=True)
            o = dot(p.astype(BF16), prefix[j, 1], ((1,), (0,))) / total
            osend[pl.ds(first, nz), j] = o.astype(BF16).reshape(nz, rows, hd)
            lse = jnp.broadcast_to(top * scale + jnp.log(total), (tile, 128))
            for b in range(tile // 128):
                lflat[j, b : b + 1, :] = jnp.transpose(lse[b * 128 : (b + 1) * 128, :])[0:1, :]

        fori(0, 2, half)
        low = lax.broadcasted_iota(jnp.int32, (1, 128), 1) < 64
        for b in range(tile // 128):
            line0, line1 = lflat[0, b : b + 1, :], lflat[1, b : b + 1, :]
            place = r * (nz // 4) + b * 2
            lsend[place] = jnp.where(low, line0, pltpu.roll(line1, 64, 1))
            lsend[place + 1] = jnp.where(low, pltpu.roll(line0, 64, 1), line1)

        def send_lse(n):
            send(lsend.at[n // 4], lin.at[n], lse_sem.at[0], lse_sem.at[1], behind(n), me_h)

        def send_back(n):
            send(osend.at[n], oin.at[n], osend_sem.at[0], osend_sem.at[1], behind(n), me_h)

        def lse_other(n):
            @pl.when(n != mine)
            def _():
                send_lse(n)

        def send_some(q, k):
            def one(i):
                n = q * nz + place_of((my_z - i) & (nz - 1))

                @pl.when(n != mine)
                def _():
                    send_back(n)

            fori(k * (nz // 4), (k + 1) * (nz // 4), one)

        fori(first, first + nz, lse_other)
        for k, late in enumerate((0, 1, 2, 1)):

            @pl.when(r >= late)
            def _(k=k, late=late):
                send_some(r - late, k)

        @pl.when(r == ny - 1)
        def _():
            for k, late in enumerate((0, 1, 2, 1)):
                fori(ny - late, ny, lambda q, k=k: send_some(q, k))

    fori(0, ny, group)
    oin[mine] = osend[mine]
    lin[mine] = lsend[mine // 4]
    wait_bytes(lin.at[pl.ds(0, serve - 1)], lse_sem.at[1])

    def weigh(c):
        for m in range(per):
            k = c * per + m
            logs = []
            for i in range(2):
                place = table_s[k, i]
                n = place >> 1
                line = jnp.broadcast_to(lin[n], (rows, 128))
                here = lanes16 == sub16 + (n & 3) * rows + (place & 1) * 64
                logs.append(jnp.sum(jnp.where(here, line, 0.0), axis=1, keepdims=True))
            own = own_lse[k]
            top = jnp.maximum(jnp.maximum(logs[0], logs[1]), own)
            a0, a1, a2 = jnp.exp(logs[0] - top), jnp.exp(logs[1] - top), jnp.exp(own - top)
            inverse = 1.0 / (a0 + a1 + a2)
            scores[k] = a0 * inverse
            own_lse[k] = a1 * inverse
            own_out[k] = own_out[k] * (a2 * inverse)

    fori(0, heads, weigh)
    wait_bytes(oin.at[pl.ds(0, serve - 1)], osend_sem.at[1])

    def mix(c, dst):
        for n in range(per):
            k = c * per + n
            p0, p1 = table_s[k, 0], table_s[k, 1]
            half0 = oin[p0 >> 1, p0 & 1].astype(F32)
            half1 = oin[p1 >> 1, p1 & 1].astype(F32)
            dst[c, n] = (scores[k] * half0 + own_lse[k] * half1 + own_out[k]).astype(BF16)

    def send_out(i):
        c = (me_h + i) & (heads - 1)
        mix(c, asend)
        send(asend.at[c], ain.at[me_h], out_sem.at[0], out_sem.at[1], me_s, c)

    fori(1, heads, send_out)
    mix(me_h, ain)
    wait_bytes(ain.at[pl.ds(0, heads - 1)], out_sem.at[1])
    for c in range(heads):
        stage[c] = ain[c].astype(F32).reshape(per * rows, hd)
    for t in range(steps):
        for c in range(heads):
            for g in range(G):
                col = (c * G + g) * hd
                out_ref[t, :, col : col + hd] = stage[
                    c, pl.ds(t * G + g, per, stride=rows), :
                ].astype(BF16)

    wait_bytes(qsend.at[pl.ds(0, serve - 1)], qsend_sem)
    wait_bytes(osend.at[pl.ds(0, serve - 1)], osend_sem.at[0])
    wait_bytes(lin.at[pl.ds(0, serve - 1)], lse_sem.at[0])
    wait_bytes(hsend.at[pl.ds(0, heads - 1)], head_sem.at[0])
    wait_bytes(fsend.at[pl.ds(0, heads - 1)], fresh_sem.at[0])
    wait_bytes(asend.at[pl.ds(0, heads - 1)], out_sem.at[0])


def local(queries, new_kv, suffix_kv, prefix_kv, owner_map, host_slot, suffix_len):
    serve, heads = lax.axis_size("serve"), lax.axis_size("head")
    steps, per = queries.shape[0], queries.shape[1]
    host, slab = suffix_kv.shape[0], prefix_kv.shape[3]
    prompts, samples = owner_map.shape[0], host_slot.shape[0]
    nz = NZ
    ny = serve // nz
    rows, hd = steps * G, 128
    cfg = (steps, per, heads, ny, nz, prompts)
    dma = pltpu.SemaphoreType.DMA
    hbm = pl.BlockSpec(memory_space=pltpu.HBM)
    return pl.pallas_call(
        functools.partial(kernel, cfg),
        out_shape=pltpu.VMEM(queries.shape, BF16),
        in_specs=[hbm] * 7,
        out_specs=pl.BlockSpec(memory_space=pltpu.VMEM),
        scratch_shapes=[
            pltpu.VMEM(queries.shape, BF16),
            pltpu.VMEM(new_kv.shape, BF16),
            pltpu.VMEM((samples // 128, 128), jnp.int32),
            pltpu.VMEM((samples // 128, 128), jnp.int32),
            pltpu.SMEM((2, prompts), jnp.int32),
            pltpu.VMEM((host, 2, 128, hd), BF16),
            pltpu.VMEM((2, 2, slab, hd), BF16),
            pltpu.VMEM((heads, per * rows, hd), F32),
            pltpu.VMEM((heads, per, rows, hd), BF16),
            pltpu.VMEM((heads, per, rows, hd), BF16),
            pltpu.VMEM((heads, 2, rows, hd), BF16),
            pltpu.VMEM((heads, 2, rows, hd), BF16),
            pltpu.VMEM((host + 8, 128), jnp.int32),
            pltpu.SMEM((host + 8, 128), jnp.int32),
            pltpu.VMEM((serve, 2, rows, hd), BF16),
            pltpu.VMEM((serve, 2, rows, hd), BF16),
            pltpu.VMEM((serve, 2, rows, hd), BF16),
            pltpu.VMEM((serve, 2, rows, hd), BF16),
            pltpu.VMEM((2, 8, 128), F32),
            pltpu.VMEM((serve // 4, 1, 128), F32),
            pltpu.VMEM((serve, 1, 128), F32),
            pltpu.VMEM((host, rows, hd), F32),
            pltpu.VMEM((host, rows, 128), F32),
            pltpu.VMEM((host, rows, 128), F32),
            pltpu.VMEM((heads, per, rows, hd), BF16),
            pltpu.VMEM((heads, per, rows, hd), BF16),
            dma((7,)),
            dma,
            dma((2,)),
            dma((2,)),
            dma((2,)),
            dma((ny,)),
            dma,
            dma((2,)),
            dma((2,)),
        ],
        compiler_params=pltpu.CompilerParams(
            collective_id=0, has_side_effects=True, vmem_limit_bytes=57 * 1024 * 1024
        ),
    )(
        queries,
        new_kv,
        host_slot.reshape(-1, 128),
        suffix_len.reshape(-1, 128),
        owner_map.T,
        suffix_kv.reshape(host, 2, 128, hd),
        prefix_kv.reshape(2, 2, slab, hd),
    )


def solution(mesh):
    return jax.shard_map(
        local,
        mesh=mesh,
        in_specs=(
            P(None, ("serve", "head"), None),
            P(None, ("serve", "head"), None),
            P("serve", "head", None, None, None),
            P("serve", "head", None, None, None),
            P(),
            P(),
            P(),
        ),
        out_specs=P(None, ("serve", "head"), None),
        check_vma=False,
    )
```

```python
import functools

import jax
import jax.numpy as jnp
from jax import lax
from jax.experimental import pallas as pl
from jax.experimental.pallas import tpu as pltpu
from jax.sharding import PartitionSpec as P

NZ = 16
G = 8
MESH = pl.DeviceIdType.MESH
F32 = jnp.float32
BF16 = jnp.bfloat16
LOG2E = 1.4426950408889634


def dot(a, b, dims):
    return lax.dot_general(a, b, (dims, ((), ())), preferred_element_type=F32)


def wait_bytes(ref, sem):
    pltpu.make_async_copy(ref, ref, sem).wait()


def kernel(
    cfg,
    q_hbm, fresh_hbm, slot_hbm, len_hbm, owner_hbm, suffix_hbm, prefix_hbm,
    out_ref,
    q_ref, fresh_ref, slot_ref, len_ref, owner_ref, suffix, prefix,
    stage, hsend, hin, fsend, fin, table_v, table_s,
    qsend, qin, osend, oin, lflat, lsend, lin,
    own_out, own_lse, scores, asend, ain,
    load_sem, table_sem, head_sem, fresh_sem, out_sem,
    qrecv_sem, qsend_sem, osend_sem, lse_sem,
):
    steps, per, heads, ny, nz, prompts = cfg
    serve = ny * nz
    host = per * heads
    hd = 128
    rows = steps * G
    far = nz // 2
    me_s = lax.axis_index("serve")
    me_h = lax.axis_index("head")
    my_y, my_z = me_s // nz, me_s % nz
    scale = hd**-0.5

    def at(y, z):
        return ((my_y + y) & (ny - 1)) * nz + ((my_z + z) & (nz - 1))

    mine = nz - 1

    def distance(n):
        i = n % nz
        if isinstance(n, int):
            return n // nz, far - (i + 1) // 2 if i % 2 == 1 else far + i // 2
        return n // nz, jnp.where(i % 2 == 1, far - (i + 1) // 2, far + i // 2)

    def place_of(z):
        return jnp.where(z < far, 2 * (far - z) - 1, 2 * (z - far))

    def ahead(n):
        return at(*distance(n))

    def behind(n):
        y, z = distance(n)
        return at(-y, -z)

    def send(src, dst, send_sem, recv_sem, s, h):
        pltpu.make_async_remote_copy(
            src_ref=src,
            dst_ref=dst,
            send_sem=send_sem,
            recv_sem=recv_sem,
            device_id=(s, h),
            device_id_type=MESH,
        ).start()

    def fori(low, high, body):
        def step(i, _):
            body(i)
            return 0

        lax.fori_loop(low, high, step, 0)

    loads = [
        pltpu.make_async_copy(src, dst, load_sem.at[i])
        for i, (src, dst) in enumerate(
            (
                (q_hbm, q_ref),
                (fresh_hbm, fresh_ref),
                (slot_hbm, slot_ref),
                (len_hbm, len_ref),
                (owner_hbm, owner_ref),
                (prefix_hbm, prefix),
                (suffix_hbm, suffix),
            )
        )
    ]
    for load in loads:
        load.start()

    barrier = pltpu.get_barrier_semaphore()

    def greet(s, h):
        pl.semaphore_signal(barrier, inc=1, device_id=(s, h), device_id_type=MESH)

    def hops(n):
        y, z = distance(n)
        return min(y, ny - y) + min(z, nz - z)

    for n in sorted(range(serve), key=hops, reverse=True):
        if n != mine:
            greet(ahead(n), me_h)
    for i in range(1, heads):
        greet(me_s, (me_h + i) & (heads - 1))

    loads[0].wait()
    for t in range(steps):
        wide = q_ref[t].astype(F32)
        for c in range(heads):
            for g in range(G):
                col = (c * G + g) * hd
                stage[c, pl.ds(t * G + g, per, stride=rows), :] = wide[:, col : col + hd]
    for c in range(heads):
        hsend[c] = stage[c].astype(BF16).reshape(per, rows, hd)
    used = per * steps
    loads[1].wait()
    for t in range(steps):
        wide = fresh_ref[t].astype(F32)
        for c in range(heads):
            for kv in range(2):
                col = (2 * c + kv) * hd
                stage[c, pl.ds(kv * rows + t, per, stride=steps), :] = wide[:, col : col + hd]
    for c in range(heads):
        for kv in range(2):
            stage[c, kv * rows + used : (kv + 1) * rows, :] = jnp.zeros((rows - used, hd), F32)
        fsend[c] = stage[c, 0 : 2 * rows, :].astype(BF16).reshape(2, rows, hd)

    for i in (2, 3, 4):
        loads[i].wait()
    lane = lax.broadcasted_iota(jnp.int32, (host, 128), 1)
    sub = lax.broadcasted_iota(jnp.int32, (host, 128), 0)
    wanted = sub + me_s * host
    found = jnp.zeros((host, 128), jnp.int32)
    for r in range(slot_ref.shape[0]):
        here = jnp.broadcast_to(slot_ref[r : r + 1, :], (host, 128)) == wanted
        held = (r * 128 + lane) // serve * 256 + jnp.broadcast_to(len_ref[r : r + 1, :], (host, 128))
        found = found + jnp.where(here, held, 0)
    found = jnp.broadcast_to(jnp.sum(found, axis=1, keepdims=True), (host, 128))
    prompt_of = found >> 8
    places, sent = [], sub * 0
    for i in range(2):
        half = sub * 0
        for p in range(prompts):
            half = jnp.where(prompt_of == p, owner_ref[i, p], half)
        sent = jnp.where(half == lane, sub, sent)
        y = ((half >> 1) // nz - my_y) & (ny - 1)
        z = ((half >> 1) - my_z) & (nz - 1)
        places.append((y * nz + place_of(z)) * 2 + (half & 1))
    table_v[0:host, :] = jnp.where(
        lane == 0, places[0], jnp.where(lane == 1, places[1], found & 255)
    )
    table_v[host : host + 8, :] = jnp.broadcast_to(jnp.max(sent, axis=0, keepdims=True), (8, 128))
    table_copy = pltpu.make_async_copy(table_v, table_s, table_sem)
    table_copy.start()

    pl.semaphore_wait(barrier, serve - 1 + heads - 1)

    def send_head(i):
        c = (me_h + i) & (heads - 1)
        send(hsend.at[c], hin.at[me_h], head_sem.at[0], head_sem.at[1], me_s, c)

    def send_fresh(i):
        c = (me_h + i) & (heads - 1)
        send(fsend.at[c], fin.at[me_h], fresh_sem.at[0], fresh_sem.at[1], me_s, c)

    fori(1, heads, send_head)
    fori(1, heads, send_fresh)
    hin[me_h] = hsend[me_h]
    fin[me_h] = fsend[me_h]
    table_copy.wait()
    wait_bytes(hin.at[pl.ds(0, heads - 1)], head_sem.at[1])

    def pick(d, j):
        k = table_s[host, d * 2 + j]
        return hin[k // per, k % per]

    def gather(shift, d):
        for j in range(2):
            qsend[shift, j] = pick(d, j)

    def send_queries(n):
        d = ahead(n)
        gather(n, d)
        send(qsend.at[n], qin.at[n], qsend_sem, qrecv_sem.at[n // nz], d, me_h)

    fori(0, mine, send_queries)
    fori(mine + 1, serve, send_queries)
    gather(mine, me_s)
    qin[mine] = qsend[mine]

    loads[6].wait()
    lanes16 = lax.broadcasted_iota(jnp.int32, (rows, 128), 1)
    sub16 = lax.broadcasted_iota(jnp.int32, (rows, 128), 0)

    def own_scores(c):
        for i in range(per):
            k = c * per + i
            s = dot(hin[c, i], suffix[k, 0], ((1,), (1,)))
            scores[k] = jnp.where(lanes16 < table_s[k, 2], s, -jnp.inf)

    fori(0, heads, own_scores)
    wait_bytes(fin.at[pl.ds(0, heads - 1)], fresh_sem.at[1])
    col = lax.broadcasted_iota(jnp.int32, (host * rows, heads * rows), 1)
    row = lax.broadcasted_iota(jnp.int32, (host * rows, heads * rows), 0)
    col_sample = col // rows * per + col % rows // steps
    live = (
        (col_sample == row // rows) & (col % rows < used) & (col % steps <= row % rows // G)
    )
    q_all = hin[...].reshape(host * rows, hd)
    fresh_k = fin[:, 0].reshape(heads * rows, hd)
    fresh_v = fin[:, 1].reshape(heads * rows, hd)
    fresh_scores = jnp.where(live, dot(q_all, fresh_k, ((1,), (1,))), -jnp.inf)
    cache_scores = scores[...].reshape(host * rows, 128)
    top = jnp.maximum(
        jnp.max(cache_scores, axis=1, keepdims=True), jnp.max(fresh_scores, axis=1, keepdims=True)
    )
    cache_exp = jnp.exp((cache_scores - top) * scale)
    fresh_exp = jnp.exp((fresh_scores - top) * scale)
    total = jnp.sum(cache_exp, axis=1, keepdims=True) + jnp.sum(fresh_exp, axis=1, keepdims=True)
    scores[...] = cache_exp.reshape(host, rows, 128)
    own_out[...] = dot(fresh_exp.astype(BF16), fresh_v, ((1,), (0,))).reshape(host, rows, hd)
    own_lse[...] = jnp.broadcast_to(top * scale + jnp.log(total), (host * rows, 128)).reshape(
        host, rows, 128
    )
    inverse = jnp.broadcast_to(1.0 / total, (host * rows, 128)).reshape(host, rows, 128)

    def own_values(c):
        for i in range(per):
            k = c * per + i
            own_out[k] = own_out[k] + dot(scores[k].astype(BF16), suffix[k, 1], ((1,), (0,)))

    fori(0, heads, own_values)
    own_out[...] = own_out[...] * inverse

    loads[5].wait()
    tile = nz * rows

    def group(r):
        @pl.when(r == 0)
        def _():
            wait_bytes(qin.at[pl.ds(0, nz - 1)], qrecv_sem.at[0])

        @pl.when(r > 0)
        def _():
            wait_bytes(qin.at[pl.ds(0, nz)], qrecv_sem.at[r])

        first = r * nz

        def half(j):
            q = qin[pl.ds(first, nz), j].reshape(tile, hd)
            s = dot(q, prefix[j, 0], ((1,), (1,)))
            top = jnp.max(s, axis=1, keepdims=True)
            p = jnp.exp2(s * (scale * LOG2E) - top * (scale * LOG2E))
            total = jnp.sum(p, axis=1, keepdims=True)
            o = dot(p.astype(BF16), prefix[j, 1], ((1,), (0,))) / total
            osend[pl.ds(first, nz), j] = o.astype(BF16).reshape(nz, rows, hd)
            lse = jnp.broadcast_to(top * scale + jnp.log(total), (tile, 128))
            for b in range(tile // 128):
                lflat[j, b : b + 1, :] = jnp.transpose(lse[b * 128 : (b + 1) * 128, :])[0:1, :]

        fori(0, 2, half)
        low = lax.broadcasted_iota(jnp.int32, (1, 128), 1) < 64
        for b in range(tile // 128):
            line0, line1 = lflat[0, b : b + 1, :], lflat[1, b : b + 1, :]
            place = r * (nz // 4) + b * 2
            lsend[place] = jnp.where(low, line0, pltpu.roll(line1, 64, 1))
            lsend[place + 1] = jnp.where(low, pltpu.roll(line0, 64, 1), line1)

        def send_lse(n):
            send(lsend.at[n // 4], lin.at[n], lse_sem.at[0], lse_sem.at[1], behind(n), me_h)

        def send_back(n):
            send(osend.at[n], oin.at[n], osend_sem.at[0], osend_sem.at[1], behind(n), me_h)

        def lse_other(n):
            @pl.when(n != mine)
            def _():
                send_lse(n)

        def send_some(q, k):
            def one(i):
                n = q * nz + place_of((my_z - i) & (nz - 1))

                @pl.when(n != mine)
                def _():
                    send_back(n)

            fori(k * (nz // 4), (k + 1) * (nz // 4), one)

        fori(first, first + nz, lse_other)
        for k, late in enumerate((0, 1, 3, 1)):

            @pl.when(r >= late)
            def _(k=k, late=late):
                send_some(r - late, k)

        @pl.when(r == ny - 1)
        def _():
            for k, late in enumerate((0, 1, 3, 1)):
                fori(ny - late, ny, lambda q, k=k: send_some(q, k))

    fori(0, ny, group)
    oin[mine] = osend[mine]
    lin[mine] = lsend[mine // 4]
    wait_bytes(lin.at[pl.ds(0, serve - 1)], lse_sem.at[1])

    def weigh(c):
        for m in range(per):
            k = c * per + m
            logs = []
            for i in range(2):
                place = table_s[k, i]
                n = place >> 1
                line = jnp.broadcast_to(lin[n], (rows, 128))
                here = lanes16 == sub16 + (n & 3) * rows + (place & 1) * 64
                logs.append(jnp.sum(jnp.where(here, line, 0.0), axis=1, keepdims=True))
            own = own_lse[k]
            top = jnp.maximum(jnp.maximum(logs[0], logs[1]), own)
            a0, a1, a2 = jnp.exp(logs[0] - top), jnp.exp(logs[1] - top), jnp.exp(own - top)
            inverse = 1.0 / (a0 + a1 + a2)
            scores[k] = a0 * inverse
            own_lse[k] = a1 * inverse
            own_out[k] = own_out[k] * (a2 * inverse)

    fori(0, heads, weigh)
    wait_bytes(oin.at[pl.ds(0, serve - 1)], osend_sem.at[1])

    def mix(c, dst):
        for n in range(per):
            k = c * per + n
            p0, p1 = table_s[k, 0], table_s[k, 1]
            half0 = oin[p0 >> 1, p0 & 1].astype(F32)
            half1 = oin[p1 >> 1, p1 & 1].astype(F32)
            dst[c, n] = (scores[k] * half0 + own_lse[k] * half1 + own_out[k]).astype(BF16)

    def send_out(i):
        c = (me_h + i) & (heads - 1)
        mix(c, asend)
        send(asend.at[c], ain.at[me_h], out_sem.at[0], out_sem.at[1], me_s, c)

    fori(1, heads, send_out)
    mix(me_h, ain)
    wait_bytes(ain.at[pl.ds(0, heads - 1)], out_sem.at[1])
    for c in range(heads):
        stage[c] = ain[c].astype(F32).reshape(per * rows, hd)
    for t in range(steps):
        for c in range(heads):
            for g in range(G):
                col = (c * G + g) * hd
                out_ref[t, :, col : col + hd] = stage[
                    c, pl.ds(t * G + g, per, stride=rows), :
                ].astype(BF16)

    wait_bytes(qsend.at[pl.ds(0, serve - 1)], qsend_sem)
    wait_bytes(osend.at[pl.ds(0, serve - 1)], osend_sem.at[0])
    wait_bytes(lin.at[pl.ds(0, serve - 1)], lse_sem.at[0])
    wait_bytes(hsend.at[pl.ds(0, heads - 1)], head_sem.at[0])
    wait_bytes(fsend.at[pl.ds(0, heads - 1)], fresh_sem.at[0])
    wait_bytes(asend.at[pl.ds(0, heads - 1)], out_sem.at[0])


def local(queries, new_kv, suffix_kv, prefix_kv, owner_map, host_slot, suffix_len):
    serve, heads = lax.axis_size("serve"), lax.axis_size("head")
    steps, per = queries.shape[0], queries.shape[1]
    host, slab = suffix_kv.shape[0], prefix_kv.shape[3]
    prompts, samples = owner_map.shape[0], host_slot.shape[0]
    nz = NZ
    ny = serve // nz
    rows, hd = steps * G, 128
    cfg = (steps, per, heads, ny, nz, prompts)
    dma = pltpu.SemaphoreType.DMA
    hbm = pl.BlockSpec(memory_space=pltpu.HBM)
    return pl.pallas_call(
        functools.partial(kernel, cfg),
        out_shape=pltpu.VMEM(queries.shape, BF16),
        in_specs=[hbm] * 7,
        out_specs=pl.BlockSpec(memory_space=pltpu.VMEM),
        scratch_shapes=[
            pltpu.VMEM(queries.shape, BF16),
            pltpu.VMEM(new_kv.shape, BF16),
            pltpu.VMEM((samples // 128, 128), jnp.int32),
            pltpu.VMEM((samples // 128, 128), jnp.int32),
            pltpu.SMEM((2, prompts), jnp.int32),
            pltpu.VMEM((host, 2, 128, hd), BF16),
            pltpu.VMEM((2, 2, slab, hd), BF16),
            pltpu.VMEM((heads, per * rows, hd), F32),
            pltpu.VMEM((heads, per, rows, hd), BF16),
            pltpu.VMEM((heads, per, rows, hd), BF16),
            pltpu.VMEM((heads, 2, rows, hd), BF16),
            pltpu.VMEM((heads, 2, rows, hd), BF16),
            pltpu.VMEM((host + 8, 128), jnp.int32),
            pltpu.SMEM((host + 8, 128), jnp.int32),
            pltpu.VMEM((serve, 2, rows, hd), BF16),
            pltpu.VMEM((serve, 2, rows, hd), BF16),
            pltpu.VMEM((serve, 2, rows, hd), BF16),
            pltpu.VMEM((serve, 2, rows, hd), BF16),
            pltpu.VMEM((2, 8, 128), F32),
            pltpu.VMEM((serve // 4, 1, 128), F32),
            pltpu.VMEM((serve, 1, 128), F32),
            pltpu.VMEM((host, rows, hd), F32),
            pltpu.VMEM((host, rows, 128), F32),
            pltpu.VMEM((host, rows, 128), F32),
            pltpu.VMEM((heads, per, rows, hd), BF16),
            pltpu.VMEM((heads, per, rows, hd), BF16),
            dma((7,)),
            dma,
            dma((2,)),
            dma((2,)),
            dma((2,)),
            dma((ny,)),
            dma,
            dma((2,)),
            dma((2,)),
        ],
        compiler_params=pltpu.CompilerParams(
            collective_id=0, has_side_effects=True, vmem_limit_bytes=57 * 1024 * 1024
        ),
    )(
        queries,
        new_kv,
        host_slot.reshape(-1, 128),
        suffix_len.reshape(-1, 128),
        owner_map.T,
        suffix_kv.reshape(host, 2, 128, hd),
        prefix_kv.reshape(2, 2, slab, hd),
    )


def solution(mesh):
    return jax.shard_map(
        local,
        mesh=mesh,
        in_specs=(
            P(None, ("serve", "head"), None),
            P(None, ("serve", "head"), None),
            P("serve", "head", None, None, None),
            P("serve", "head", None, None, None),
            P(),
            P(),
            P(),
        ),
        out_specs=P(None, ("serve", "head"), None),
        check_vma=False,
    )
```
